32 devices in a mesh: parts: 2 (over x), gx: 16 (over z, y, core).
Axes of the slice: x: 2, y: 2, z: 4, core: 2. Of those that a mesh axis runs over, the one named last changes fastest.
Arguments:
- features: bfloat16 [16384, 256], P(('parts', 'gx')), parts along dimension 0, may hold values from -6 to 6
- neighbours: int32 [27, 16384], P(None, ('parts', 'gx')), parts along dimension 1, may hold values from 0 to 640, as said below
- rim_rows: int32 [4096], P(('parts', 'gx')), parts along dimension 0, may hold values from 0 to 511, as said below
- tile_slot: int32 [16384], P(('parts', 'gx')), parts along dimension 0, may hold values from 0 to 1023, as said below
- patch_rows: int32 [16384], P(('parts', 'gx')), parts along dimension 0, may hold values from 0 to 1023, as said below
- conv_weight: bfloat16 [6912, 256], replicated, may hold values from -0.078125 to 0.078125
- norm_gain: float32 [256], replicated, may hold values from 0.1 to 1.9
- qkv_weight: bfloat16 [256, 768], replicated
- proj_weight: bfloat16 [256, 256], replicated, may hold values from -0.375 to 0.375
- out_grad: bfloat16 [16384, 256], P(('parts', 'gx')), parts along dimension 0, may hold values from -6 to 6
Outputs:
- block_out: bfloat16 [16384, 256], P(('parts', 'gx')), parts along dimension 0
- conv_grad: float32 [13824, 256], P(('parts', 'gx')), parts along dimension 0
- qkv_grad: float32 [512, 768], P(('parts', 'gx')), parts along dimension 0
- proj_grad: float32 [512, 256], P(('parts', 'gx')), parts along dimension 0
- gain_grad: float32 [512], P(('parts', 'gx')), parts along dimension 0
The draws below stay inside these ranges and needn't reach their ends.
There are 2 independent parts, one for each index of `parts`. The reference program is written for one: setup_inputs(seed, part) draws one part's arguments, and reference() takes and returns one part's arrays. A program takes and returns all parts, laid end to end along the dimension named above; an argument that names none is the same for every part. Nothing has to cross between parts.
Inputs may be any that keep to these rules, and one draw needn't show every extreme that they name: `tile_slot`: value // 64 is the owner tile of the point's patch, value % 64 its slot; a tile's entries are distinct; at most 64 points of one tile go to one patch, exactly 64 for some pair in every draw; every patch receives exactly 512 points. `patch_rows`: A patch's 512 entries are distinct and are exactly the slots t * 64 + s filled for it by the tiles. `neighbours`: rows 0 to 511 of a tile's table are its points, the next 64 come from the previous tile, the next 64 from the next tile; 640 means no neighbour; offset 13 is the point itself. `rim_rows`: per tile 2 * 64 distinct rows: first those sent to the previous tile, then those sent to the next.
All inputs are finite; a program needn't handle non-finite values.
Results may differ from the reference program's by a relative error of at most 0.012.
The reference program's roundings to bfloat16 on the way count: a program that leaves them out, or rounds other values in their place, can miss the bound.
Values may be sent and summed in bfloat16 or wider, within the bound.
A program may use at most 128 MiB of HBM per device.

```python
import jax
import jax.numpy as jnp
from jax import lax

C = 256
HEADS = 16
HEAD = 16
KERNEL = 27
PATCH = 512
RIM = 64
TILES = 16
POINTS = 8192
CAP = 64


def regroup_lists(key):
    per_pair = PATCH // TILES
    spread = per_pair // 2
    first = jax.random.fold_in(key, 0)
    fourth = jax.random.fold_in(key, 3)
    fifth = jax.random.fold_in(key, 4)
    excess = jax.random.randint(first, (TILES, TILES), 0, spread + 1)
    tile_pick = TILES - 1
    offset_pick = 0
    excess = excess.at[tile_pick, offset_pick].set(spread)
    excess = excess.at[(tile_pick - 1) % TILES, offset_pick].set(spread)
    excess = excess.at[tile_pick, (offset_pick - 1) % TILES].set(0)
    excess = excess.at[(tile_pick - 1) % TILES, (offset_pick + 1) % TILES].set(0)
    previous = jnp.roll(excess, 1, axis=0)
    load = per_pair + excess - jnp.roll(excess, 1, axis=1) - jnp.roll(previous, -1, axis=1) + previous
    tile_ids = jnp.arange(TILES, dtype=jnp.int32)
    offsets = (tile_ids[None, :] - tile_ids[:, None]) % TILES
    counts = jnp.take_along_axis(load, offsets, axis=1)
    ending = jnp.cumsum(counts, axis=1)
    starting = ending - counts
    tile_keys = jax.random.split(fourth, TILES)
    ranks = jax.vmap(lambda one_key: jnp.argsort(jax.random.permutation(one_key, PATCH)))(tile_keys)
    owner = jnp.sum((ranks[:, :, None] >= ending[:, None, :]).astype(jnp.int32), axis=2)
    slot = ranks - jnp.take_along_axis(starting, owner, axis=1)
    tile_slot = (owner * CAP + slot).reshape(-1)
    filled = counts.T[:, :, None] > jnp.arange(CAP, dtype=jnp.int32)[None, None, :]
    filled = filled.reshape(TILES, TILES * CAP)
    owner_keys = jax.random.split(fifth, TILES)
    shuffled = jax.vmap(lambda one_key: jax.random.permutation(one_key, TILES * CAP))(owner_keys)
    score = jnp.where(filled, shuffled, TILES * CAP + shuffled)
    patch_rows = jnp.argsort(score, axis=1)[:, :PATCH].reshape(-1)
    return (tile_slot.astype(jnp.int32), patch_rows.astype(jnp.int32))


def draw_tile_slot(key, part):
    tile_slot, patch_rows = regroup_lists(key)
    return tile_slot


def draw_patch_rows(key, part):
    tile_slot, patch_rows = regroup_lists(key)
    return patch_rows


def draw_neighbours(key, part):
    key = jax.random.fold_in(key, 7)
    first, second = jax.random.split(key)
    empty_row = PATCH + 2 * RIM
    picks = jax.random.randint(first, (KERNEL, TILES * PATCH), 0, empty_row)
    occupied = jax.random.randint(second, (KERNEL, TILES * PATCH), 0, 10) < 4
    centre = jnp.arange(TILES * PATCH, dtype=jnp.int32) % PATCH
    lists = jnp.where(occupied, picks, empty_row)
    lists = lists.at[KERNEL // 2].set(centre)
    return lists.astype(jnp.int32)


def draw_rim_rows(key, part):
    key = jax.random.fold_in(key, 9)
    tile_keys = jax.random.split(key, TILES)
    chosen = jax.vmap(lambda one_key: jax.random.permutation(one_key, PATCH)[:2 * RIM])(tile_keys)
    return chosen.reshape(-1).astype(jnp.int32)


def draw_qkv_weight(key, part):
    key = jax.random.fold_in(key, 5)
    first = jax.random.fold_in(key, 0)
    matrix = jax.random.normal(first, (C, 3 * C), jnp.float32) * C ** (-0.5)
    return matrix.astype(jnp.bfloat16)


def level_of(key, shape, cuts, low, top_value):
    level, own = 1.0, jax.random.fold_in(key, 6)
    for dim, blocks in cuts:
        steps = jnp.exp(jax.random.uniform(jax.random.fold_in(own, dim), (blocks,), jnp.float32, low / len(cuts), top_value / len(cuts)))
        level = level * jnp.repeat(steps, shape[dim] // blocks).reshape([-1 if axis == dim else 1 for axis in range(len(shape))])
    return level


def gaussian(stream_key, dims, deviation, bound, shards=(), held_as=jnp.bfloat16):
    drawn = jax.random.normal(stream_key, dims, jnp.float32) * deviation
    if len(shards) > 0:
        drawn = level_of(stream_key, dims, shards, -0.22, 0.18) * drawn
    return jnp.clip(drawn, min=-bound, max=bound).astype(held_as)


def setup_inputs(seed: int = 0, part: int = 0) -> dict:
    splits = jax.random.split(jax.random.key(seed), 11)
    own_keys = jax.random.split(jax.random.fold_in(splits[10], part), 11)
    features = gaussian(own_keys[0], (POINTS, C), 1.0, 6.0, ((0, 16),))
    neighbours = draw_neighbours(jax.random.fold_in(jax.random.fold_in(splits[10], part), 71), part)
    rim_rows = draw_rim_rows(jax.random.fold_in(jax.random.fold_in(splits[10], part), 71), part)
    tile_slot = draw_tile_slot(jax.random.fold_in(jax.random.fold_in(splits[10], part), 71), part)
    patch_rows = draw_patch_rows(jax.random.fold_in(jax.random.fold_in(splits[10], part), 71), part)
    conv_weight = gaussian(splits[5], (KERNEL * C, C), (KERNEL * C) ** -0.5, 0.078125)
    norm_gain = jnp.clip(1.0 + 0.18 * jax.random.normal(splits[6], (C,), jnp.float32), 0.1, 1.9)
    qkv_weight = draw_qkv_weight(jax.random.fold_in(splits[10], 71), part)
    proj_weight = gaussian(splits[8], (C, C), C ** -0.5, 0.375)
    out_grad = gaussian(own_keys[9], (POINTS, C), 1.0, 6.0, ((0, 16),))
    return {"features": features, "neighbours": neighbours, "rim_rows": rim_rows, "tile_slot": tile_slot, "patch_rows": patch_rows, "conv_weight": conv_weight, "norm_gain": norm_gain, "qkv_weight": qkv_weight, "proj_weight": proj_weight, "out_grad": out_grad}


def softmax_rows(scores):
    highest = lax.optimization_barrier(jnp.max(scores, axis=-1, keepdims=True))
    raised = jnp.exp(scores - highest)
    return raised / lax.optimization_barrier(jnp.sum(raised, axis=-1, keepdims=True))

def patch_pass(patch_in, patch_grad, qkv_weight, proj_weight):
    length = patch_in.shape[0]
    scaling = HEAD ** (-0.5)
    qkv = jnp.dot(patch_in, qkv_weight, preferred_element_type=jnp.float32).astype(jnp.bfloat16)
    query = qkv[:, :C].reshape(length, HEADS, HEAD).astype(jnp.float32)
    keys = qkv[:, C:2 * C].reshape(length, HEADS, HEAD).astype(jnp.float32)
    values = qkv[:, 2 * C:].reshape(length, HEADS, HEAD).astype(jnp.float32)
    probs = softmax_rows(jnp.einsum('qhd,khd->hqk', query, keys) * scaling)
    probs_low = probs.astype(jnp.bfloat16).astype(jnp.float32)
    attended = jnp.einsum('hqk,khd->qhd', probs_low, values).reshape(length, C).astype(jnp.bfloat16)
    proj_out = jnp.dot(attended, proj_weight, preferred_element_type=jnp.float32).astype(jnp.bfloat16)
    proj_term = lax.dot_general(attended, patch_grad, (((0,), (0,)), ((), ())), preferred_element_type=jnp.float32)
    upstream = lax.dot_general(patch_grad, proj_weight, (((1,), (1,)), ((), ())), preferred_element_type=jnp.float32)
    upstream = upstream.astype(jnp.bfloat16).reshape(length, HEADS, HEAD).astype(jnp.float32)
    grad_vals = jnp.einsum('hqk,qhd->khd', probs_low, upstream)
    grad_probs = jnp.einsum('qhd,khd->hqk', upstream, values)
    row_total = lax.optimization_barrier(jnp.sum(grad_probs * probs, axis=-1, keepdims=True))
    grad_scores = (probs * (grad_probs - row_total) * scaling).astype(jnp.bfloat16).astype(jnp.float32)
    grad_query = jnp.einsum('hqk,khd->qhd', grad_scores, keys)
    grad_keys = jnp.einsum('hqk,qhd->khd', grad_scores, query)
    grad_qkv = jnp.concatenate([grad_query.reshape(length, C), grad_keys.reshape(length, C), grad_vals.reshape(length, C)], axis=1).astype(jnp.bfloat16)
    qkv_term = lax.dot_general(patch_in, grad_qkv, (((0,), (0,)), ((), ())), preferred_element_type=jnp.float32)
    grad_normed = lax.dot_general(grad_qkv, qkv_weight, (((1,), (1,)), ((), ())), preferred_element_type=jnp.float32).astype(jnp.bfloat16)
    return (proj_out, grad_normed, qkv_term, proj_term)

def reference(features, neighbours, rim_rows, tile_slot, patch_rows, conv_weight, norm_gain, qkv_weight, proj_weight, out_grad):
    tiled = features.reshape(TILES, PATCH, C)
    rim_index = rim_rows.reshape(TILES, 2 * RIM)
    rim_feats = jnp.take_along_axis(tiled, rim_index[:, :, None], axis=1)
    zero_rim = jnp.zeros((1, RIM, C), jnp.bfloat16)
    from_left = jnp.concatenate([zero_rim, rim_feats[:-1, RIM:]], axis=0)
    from_right = jnp.concatenate([rim_feats[1:, :RIM], zero_rim], axis=0)
    table = jnp.concatenate([tiled, from_left, from_right, jnp.zeros((TILES, 1, C), jnp.bfloat16)], axis=1)
    lists = neighbours.reshape(KERNEL, TILES, PATCH).transpose(1, 2, 0)
    gathered = jax.vmap(lambda rows_table, rows_list: rows_table[rows_list])(table, lists)
    gathered = gathered.reshape(TILES * PATCH, KERNEL * C)
    hidden = features.astype(jnp.float32) + jnp.dot(gathered, conv_weight, preferred_element_type=jnp.float32)
    row_mean = lax.optimization_barrier(jnp.mean(hidden, axis=-1, keepdims=True))
    centred = hidden - row_mean
    inv_std = 1.0 / jnp.sqrt(lax.optimization_barrier(jnp.mean(centred * centred, axis=-1, keepdims=True)) + 1e-05)
    standard = centred * inv_std
    normed = (standard * norm_gain).astype(jnp.bfloat16)
    slots = tile_slot.reshape(TILES, PATCH)
    owner = slots // CAP
    position = jnp.arange(TILES, dtype=jnp.int32)[:, None] * CAP + slots % CAP
    patch_index = patch_rows.reshape(TILES, PATCH)
    owner_ids = jnp.arange(TILES, dtype=jnp.int32)[:, None]

    def to_owners(values):
        buffer = jnp.zeros((TILES, TILES * CAP, C), values.dtype).at[owner, position].set(values.reshape(TILES, PATCH, C))
        return jnp.take_along_axis(buffer, patch_index[:, :, None], axis=1)

    def to_tiles(values):
        buffer = jnp.zeros((TILES, TILES * CAP, C), values.dtype).at[owner_ids, patch_index].set(values)
        return buffer[owner, position].reshape(TILES * PATCH, C)
    patch_in = to_owners(normed)
    patch_grad = to_owners(out_grad)
    proj_out, grad_normed, qkv_terms, proj_terms = lax.map(lambda pieces: patch_pass(pieces[0], pieces[1], qkv_weight, proj_weight), (patch_in, patch_grad))
    returned = to_tiles(proj_out).astype(jnp.float32)
    block_out = (hidden + returned).astype(jnp.bfloat16)
    grad_back = to_tiles(grad_normed).astype(jnp.float32)
    gain_grad = lax.optimization_barrier(jnp.sum(grad_back * standard, axis=0))
    scaled = grad_back * norm_gain
    grad_hidden = out_grad.astype(jnp.float32) + inv_std * (scaled - lax.optimization_barrier(jnp.mean(scaled, axis=-1, keepdims=True)) - standard * lax.optimization_barrier(jnp.mean(scaled * standard, axis=-1, keepdims=True)))
    grad_hidden = grad_hidden.astype(jnp.bfloat16)
    conv_grad = lax.dot_general(gathered, grad_hidden, (((0,), (0,)), ((), ())), preferred_element_type=jnp.float32)
    return (block_out, conv_grad, lax.optimization_barrier(jnp.sum(qkv_terms, axis=0)), lax.optimization_barrier(jnp.sum(proj_terms, axis=0)), gain_grad)
```

```python
import functools

import jax
import jax.numpy as jnp
from jax import lax
from jax.experimental import pallas as pl
from jax.experimental.pallas import tpu as pltpu
from jax.sharding import PartitionSpec as P

HEADS = 16
HEAD = 16
LIMIT = 56 * 1024 * 1024
F32 = jnp.float32
BF16 = jnp.bfloat16
VMEM = pl.BlockSpec(memory_space=pltpu.VMEM)


def dot(a, b, ca=1, cb=0):
    return lax.dot_general(a, b, (((ca,), (cb,)), ((), ())), preferred_element_type=F32)


def hot_rows(index_row, count):
    rows = lax.broadcasted_iota(jnp.int32, (count, index_row.shape[1]), 0)
    return jnp.where(rows == index_row, 1.0, 0.0).astype(BF16)


def hot_columns(index_column, count):
    columns = lax.broadcasted_iota(jnp.int32, (index_column.shape[0], count), 1)
    return jnp.where(columns == index_column, 1.0, 0.0).astype(BF16)


def normalise(hidden):
    centred = hidden - jnp.mean(hidden, axis=-1, keepdims=True)
    inv_std = 1.0 / jnp.sqrt(jnp.mean(centred * centred, axis=-1, keepdims=True) + 1e-05)
    return centred * inv_std, inv_std


def start_kernel(feats, grads, rim_col, slot_row, rim_out, slots_out):
    rim_out[...] = dot(hot_columns(rim_col[...], feats.shape[0]), feats[...]).astype(BF16)
    slots_out[...] = dot(hot_rows(slot_row[...], slots_out.shape[0]), grads[...]).astype(BF16)


def conv_kernel(
    feats, low, high, nbrs, weight, gain, slot_row, gathered_out, hidden_out, slots_out, table, acc
):
    k = pl.program_id(0)
    rows = feats.shape[0]
    rim = low.shape[0]

    @pl.when(k == 0)
    def _():
        table[:, :rows] = feats[...].T
        table[:, rows : rows + rim] = low[...].T
        table[:, rows + rim :] = high[...].T
        acc[...] = jnp.zeros_like(acc)

    gathered = dot(table[...], hot_rows(nbrs[0], rows + 2 * rim)).astype(BF16)
    gathered_out[0] = gathered
    acc[...] += dot(weight[...], gathered, 0, 0)

    @pl.when(k == pl.num_programs(0) - 1)
    def _():
        hidden = feats[...].astype(F32) + acc[...].T
        hidden_out[...] = hidden
        standard, _ = normalise(hidden)
        normed = (standard * gain[...]).astype(BF16)
        slots_out[...] = dot(hot_rows(slot_row[...], slots_out.shape[0]), normed).astype(BF16)


def attention_kernel(
    recv_normed, recv_grad, rows_row, rows_col, qkv_w, proj_w,
    out_proj, out_grad, qkv_term, proj_term,
    qkv_t, scaled_t, up_t, att_t, grad_t,
):
    channels = proj_w.shape[0]
    slots = recv_normed.shape[0]
    picks = hot_columns(rows_col[...], slots)
    patch_in = dot(picks, recv_normed[...]).astype(BF16)
    patch_grad = dot(picks, recv_grad[...]).astype(BF16)
    qkv = dot(patch_in, qkv_w[...]).T
    qkv_t[...] = qkv.astype(BF16)
    scaled_t[...] = (qkv_t[:channels, :].astype(F32) * 0.25).astype(BF16)
    up_t[...] = dot(patch_grad, proj_w[...], 1, 1).T.astype(BF16)

    def head(h, carry):
        def part(ref, base=0):
            return ref[pl.ds(pl.multiple_of(base + h * HEAD, HEAD), HEAD), :]

        query, keys, values = part(qkv_t), part(qkv_t, channels), part(qkv_t, 2 * channels)
        query_low = part(scaled_t)
        up = part(up_t)
        up_low = (up.astype(F32) * 0.25).astype(BF16)
        scores = dot(keys, query_low, 0, 0)
        raised = jnp.exp(scores - jnp.max(scores, axis=0, keepdims=True))
        probs = raised * (1.0 / jnp.sum(raised, axis=0, keepdims=True))
        probs_low = probs.astype(BF16)
        grad_probs = dot(values, up_low, 0, 0)
        total = jnp.sum(grad_probs * probs, axis=0, keepdims=True)
        grad_scores = (probs * (grad_probs - total)).astype(BF16)

        def put(ref, value, base=0):
            ref[pl.ds(pl.multiple_of(base + h * HEAD, HEAD), HEAD), :] = value.astype(BF16)

        put(att_t, dot(values, probs_low))
        put(grad_t, dot(up, probs_low, 1, 1), 2 * channels)
        put(grad_t, dot(keys, grad_scores))
        put(grad_t, dot(query, grad_scores, 1, 1), channels)
        return carry

    lax.fori_loop(0, HEADS, head, 0, unroll=2)
    back = hot_rows(rows_row[...], slots)
    proj_out = dot(att_t[...], proj_w[...], 0, 0).astype(BF16)
    out_proj[...] = dot(back, proj_out).astype(BF16)
    proj_term[...] = dot(att_t[...], patch_grad)
    grad_qkv = grad_t[...].astype(F32).T.astype(BF16)
    qkv_term[...] = dot(patch_in, grad_qkv, 0, 0)
    grad_normed = dot(grad_qkv, qkv_w[...], 1, 1).astype(BF16)
    out_grad[...] = dot(back, grad_normed).astype(BF16)


def backward_kernel(
    hidden, back_proj, back_grad, out_grad, gain, slot_col, gathered,
    block_out, gain_term, conv_term, grad_hidden,
):
    @pl.when(pl.program_id(0) == 0)
    def _():
        picks = hot_columns(slot_col[...], back_proj.shape[0])
        value = hidden[...]
        block_out[...] = (value + dot(picks, back_proj[...])).astype(BF16)
        grad_back = dot(picks, back_grad[...])
        standard, inv_std = normalise(value)
        gain_term[...] = jnp.sum(grad_back * standard, axis=0, keepdims=True)
        scaled = grad_back * gain[...]
        grad_hidden[...] = (
            out_grad[...].astype(F32)
            + inv_std
            * (
                scaled
                - jnp.mean(scaled, axis=-1, keepdims=True)
                - standard * jnp.mean(scaled * standard, axis=-1, keepdims=True)
            )
        ).astype(BF16)

    conv_term[...] = dot(gathered[0], grad_hidden[...])


def reduce_kernel(
    count, conv, small, conv_out, small_out,
    near_conv, near_small, send_conv, send_small, far_conv, far_small,
    near_send, near_recv, far_send, far_recv,
):
    me = lax.axis_index("gx")
    core = lax.rem(me, 2)
    chip = me // 2
    chips = count // 2
    sibling = chip * 2 + 1 - core
    order = [lax.rem(chip + step, chips) for step in range(1, chips + 1)]
    barrier = pltpu.get_barrier_semaphore()
    pl.semaphore_signal(
        barrier, inc=1, device_id={"gx": sibling}, device_id_type=pl.DeviceIdType.MESH
    )
    for peer in order[:-1]:
        pl.semaphore_signal(
            barrier, inc=1, device_id={"gx": peer * 2 + core}, device_id_type=pl.DeviceIdType.MESH
        )
    pl.semaphore_wait(barrier, chips)

    def copy(source, target, send, recv, device):
        return pltpu.make_async_remote_copy(
            src_ref=source,
            dst_ref=target,
            send_sem=send,
            recv_sem=recv,
            device_id={"gx": device},
            device_id_type=pl.DeviceIdType.MESH,
        )

    near = []
    for step, peer in enumerate(order):
        theirs = peer * 2 + 1 - core
        near.append(
            (
                copy(conv.at[theirs], near_conv.at[step], near_send.at[2 * step],
                     near_recv.at[2 * step], sibling),
                copy(small.at[theirs], near_small.at[step], near_send.at[2 * step + 1],
                     near_recv.at[2 * step + 1], sibling),
            )
        )
        for one in near[-1]:
            one.start()
    far = []
    for step, peer in enumerate(order):
        mine = peer * 2 + core
        for one in near[step]:
            one.wait_recv()
        conv_sum = conv[mine] + near_conv[step]
        small_sum = small[mine] + near_small[step]
        if step < chips - 1:
            send_conv[step] = conv_sum.astype(BF16)
            send_small[step] = small_sum.astype(BF16)
            far.append(
                (
                    copy(send_conv.at[step], far_conv.at[step], far_send.at[2 * step],
                         far_recv.at[2 * step], mine),
                    copy(send_small.at[step], far_small.at[step], far_send.at[2 * step + 1],
                         far_recv.at[2 * step + 1], mine),
                )
            )
            for one in far[-1]:
                one.start()
        else:
            conv_out[...] = conv_sum
            small_out[...] = small_sum
    for step in range(chips - 1):
        for one in far[step]:
            one.wait_recv()
        conv_out[...] += far_conv[step].astype(F32)
        small_out[...] += far_small[step].astype(F32)
    for pair in near:
        for one in pair:
            one.wait_send()
    for pair in far:
        for one in pair:
            one.wait_send()


def params(**more):
    return pltpu.CompilerParams(vmem_limit_bytes=LIMIT, **more)


def shape(dims, dtype):
    return jax.ShapeDtypeStruct(dims, dtype)


def on_device(
    features,
    neighbours,
    rim_rows,
    tile_slot,
    patch_rows,
    conv_weight,
    norm_gain,
    qkv_weight,
    proj_weight,
    out_grad,
):
    rows, channels = features.shape
    count = lax.axis_size("gx")
    capacity = 2 * rows // count
    slots = count * capacity
    rim = rim_rows.shape[0] // 2
    kernel = neighbours.shape[0]
    gain = norm_gain.reshape(1, channels)
    slot_row, slot_col = tile_slot.reshape(1, rows), tile_slot.reshape(rows, 1)
    rows_row, rows_col = patch_rows.reshape(1, rows), patch_rows.reshape(rows, 1)

    rim_feats, grad_slots = pl.pallas_call(
        start_kernel,
        out_shape=(shape((2 * rim, channels), BF16), shape((slots, channels), BF16)),
        in_specs=[VMEM] * 4,
        out_specs=(VMEM, VMEM),
        compiler_params=params(),
        name="start",
    )(features, out_grad, rim_rows.reshape(2 * rim, 1), slot_row)
    forward = [(i, i + 1) for i in range(count - 1)]
    backward = [(target, source) for source, target in forward]
    low = lax.ppermute(rim_feats[rim:], "gx", forward)
    high = lax.ppermute(rim_feats[:rim], "gx", backward)

    def swap(values):
        return lax.all_to_all(
            values.reshape(count, capacity, -1), "gx", split_axis=0, concat_axis=0, tiled=True
        ).reshape(slots, -1)

    recv_grad = swap(grad_slots)

    def full(*dims):
        return pl.BlockSpec(dims, lambda k: (0,) * len(dims))

    gathered, hidden, normed_slots = pl.pallas_call(
        conv_kernel,
        grid=(kernel,),
        out_shape=(
            shape((kernel, channels, rows), BF16),
            shape((rows, channels), F32),
            shape((slots, channels), BF16),
        ),
        in_specs=[
            full(rows, channels),
            full(rim, channels),
            full(rim, channels),
            pl.BlockSpec((1, 1, rows), lambda k: (k, 0, 0)),
            pl.BlockSpec((channels, channels), lambda k: (k, 0)),
            full(1, channels),
            full(1, rows),
        ],
        out_specs=(
            pl.BlockSpec((1, channels, rows), lambda k: (k, 0, 0)),
            full(rows, channels),
            full(slots, channels),
        ),
        scratch_shapes=[
            pltpu.VMEM((channels, rows + 2 * rim), BF16),
            pltpu.VMEM((channels, rows), F32),
        ],
        compiler_params=params(),
        name="conv",
    )(features, low, high, neighbours.reshape(kernel, 1, rows), conv_weight, gain, slot_row)
    recv_normed = swap(normed_slots)

    proj_slots, grad_normed_slots, qkv_term, proj_term = pl.pallas_call(
        attention_kernel,
        out_shape=(
            shape((slots, channels), BF16),
            shape((slots, channels), BF16),
            shape((channels, 3 * channels), F32),
            shape((channels, channels), F32),
        ),
        in_specs=[VMEM] * 6,
        out_specs=(VMEM,) * 4,
        scratch_shapes=[
            pltpu.VMEM((3 * channels, rows), BF16),
            pltpu.VMEM((channels, rows), BF16),
            pltpu.VMEM((channels, rows), BF16),
            pltpu.VMEM((channels, rows), BF16),
            pltpu.VMEM((3 * channels, rows), BF16),
        ],
        compiler_params=params(),
        name="attention",
    )(recv_normed, recv_grad, rows_row, rows_col, qkv_weight, proj_weight)

    back_grad = swap(grad_normed_slots)
    back_proj = swap(proj_slots)

    block_out, gain_term, conv_term = pl.pallas_call(
        backward_kernel,
        grid=(kernel,),
        out_shape=(
            shape((rows, channels), BF16),
            shape((1, channels), F32),
            shape((kernel * channels, channels), F32),
        ),
        in_specs=[
            full(rows, channels),
            full(slots, channels),
            full(slots, channels),
            full(rows, channels),
            full(1, channels),
            full(rows, 1),
            pl.BlockSpec((1, channels, rows), lambda k: (k, 0, 0)),
        ],
        out_specs=(
            full(rows, channels),
            full(1, channels),
            pl.BlockSpec((channels, channels), lambda k: (k, 0)),
        ),
        scratch_shapes=[pltpu.VMEM((rows, channels), BF16)],
        compiler_params=params(),
        name="backward",
    )(hidden, back_proj, back_grad, out_grad, gain, slot_col, gathered)

    conv_rows = kernel * channels // count
    one = channels // count
    used = 4 * one + 1
    small_rows = -(-used // 16) * 16
    small = jnp.concatenate(
        [
            qkv_term.reshape(count, 3 * one, channels),
            proj_term.reshape(count, one, channels),
            jnp.pad(
                gain_term.reshape(count, 1, one),
                ((0, 0), (0, small_rows - used), (0, channels - one)),
            ),
        ],
        axis=1,
    )
    small = jnp.pad(small, ((0, 0), (0, small_rows - small.shape[1]), (0, 0)))
    chips = count // 2
    conv_rows_pad = -(-conv_rows // 16) * 16
    conv_term = conv_term.reshape(count, conv_rows, channels)
    if conv_rows_pad > conv_rows:
        conv_term = jnp.pad(conv_term, ((0, 0), (0, conv_rows_pad - conv_rows), (0, 0)))
    conv_grad, small_sum = pl.pallas_call(
        functools.partial(reduce_kernel, count),
        out_shape=(shape((conv_rows_pad, channels), F32), shape((small_rows, channels), F32)),
        in_specs=[VMEM] * 2,
        out_specs=(VMEM, VMEM),
        scratch_shapes=[
            pltpu.VMEM((chips, conv_rows_pad, channels), F32),
            pltpu.VMEM((chips, small_rows, channels), F32),
            pltpu.VMEM((chips - 1, conv_rows_pad, channels), BF16),
            pltpu.VMEM((chips - 1, small_rows, channels), BF16),
            pltpu.VMEM((chips - 1, conv_rows_pad, channels), BF16),
            pltpu.VMEM((chips - 1, small_rows, channels), BF16),
            pltpu.SemaphoreType.DMA((2 * chips,)),
            pltpu.SemaphoreType.DMA((2 * chips,)),
            pltpu.SemaphoreType.DMA((2 * chips,)),
            pltpu.SemaphoreType.DMA((2 * chips,)),
        ],
        compiler_params=params(collective_id=1, has_side_effects=True),
        name="reduce",
    )(conv_term, small)
    return (
        block_out,
        conv_grad[:conv_rows],
        small_sum[: 3 * one].reshape(one, 3 * channels),
        small_sum[3 * one : 4 * one],
        small_sum[4 * one, :one],
    )


def solution(mesh):
    placed = (
        P(("parts", "gx"), None),
        P(None, ("parts", "gx")),
        P(("parts", "gx")),
        P(("parts", "gx")),
        P(("parts", "gx")),
        P(),
        P(),
        P(),
        P(),
        P(("parts", "gx"), None),
    )
    return jax.shard_map(
        on_device,
        mesh=mesh,
        in_specs=placed,
        out_specs=(
            P(("parts", "gx"), None),
            P(("parts", "gx"), None),
            P(("parts", "gx"), None),
            P(("parts", "gx"), None),
            P(("parts", "gx")),
        ),
        check_vma=False,
    )
```

```python
import functools

import jax
import jax.numpy as jnp
from jax import lax
from jax.experimental import pallas as pl
from jax.experimental.pallas import tpu as pltpu
from jax.sharding import PartitionSpec as P

HEADS = 16
HEAD = 16
LIMIT = 56 * 1024 * 1024
F32 = jnp.float32
BF16 = jnp.bfloat16
VMEM = pl.BlockSpec(memory_space=pltpu.VMEM)


def dot(a, b, ca=1, cb=0):
    return lax.dot_general(a, b, (((ca,), (cb,)), ((), ())), preferred_element_type=F32)


def hot_rows(index_row, count):
    rows = lax.broadcasted_iota(jnp.int32, (count, index_row.shape[1]), 0)
    return jnp.where(rows == index_row, 1.0, 0.0).astype(BF16)


def hot_columns(index_column, count):
    columns = lax.broadcasted_iota(jnp.int32, (index_column.shape[0], count), 1)
    return jnp.where(columns == index_column, 1.0, 0.0).astype(BF16)


def normalise(hidden):
    centred = hidden - jnp.mean(hidden, axis=-1, keepdims=True)
    inv_std = 1.0 / jnp.sqrt(jnp.mean(centred * centred, axis=-1, keepdims=True) + 1e-05)
    return centred * inv_std, inv_std


def copy_to(source, target, send, recv, device):
    return pltpu.make_async_remote_copy(
        src_ref=source,
        dst_ref=target,
        send_sem=send,
        recv_sem=recv,
        device_id={"gx": device},
        device_id_type=pl.DeviceIdType.MESH,
    )


def greet(devices):
    barrier = pltpu.get_barrier_semaphore()
    for device in devices:
        pl.semaphore_signal(
            barrier, inc=1, device_id={"gx": device}, device_id_type=pl.DeviceIdType.MESH
        )
    pl.semaphore_wait(barrier, len(devices))


class Exchange:
    def __init__(self, count, me, source, target, send, recv):
        self.own = pltpu.make_async_copy(source.at[me], target.at[me], send.at[0])
        self.sends = []
        self.recvs = []
        for step in range(1, count):
            peer = lax.rem(me + step, count)
            sender = lax.rem(me + count - step, count)
            self.sends.append(
                copy_to(source.at[peer], target.at[me], send.at[step], recv.at[step], peer)
            )
            self.recvs.append(
                copy_to(source.at[peer], target.at[sender], send.at[step], recv.at[step], peer)
            )

    def start(self):
        for one in self.sends:
            one.start()
        self.own.start()

    def arrive(self):
        self.own.wait()
        for one in self.recvs:
            one.wait_recv()

    def leave(self):
        for one in self.sends:
            one.wait_send()


def put_slots(target, values):
    for block in range(target.shape[0]):
        cap = target.shape[1]
        target[block] = values[block * cap : (block + 1) * cap]


def conv_kernel(
    count, feats, grads, rim_col, nbrs, weight, gain, slot_row,
    gathered_out, hidden_out, recv_normed, recv_grad,
    table, acc, rim_send, rim_recv, grad_slots, normed_slots,
    rim_out, rim_in, grad_out, grad_in, normed_out, normed_in,
):
    k = pl.program_id(0)
    rows, channels = feats.shape
    rim = rim_recv.shape[1]
    slots = count * grad_slots.shape[1]
    me = lax.axis_index("gx")
    before, after = lax.rem(me + count - 1, count), lax.rem(me + 1, count)
    to_before = copy_to(rim_send.at[0], rim_recv.at[1], rim_out.at[0], rim_in.at[1], before)
    to_after = copy_to(rim_send.at[1], rim_recv.at[0], rim_out.at[1], rim_in.at[0], after)
    grad_swap = Exchange(count, me, grad_slots, recv_grad, grad_out, grad_in)
    normed_swap = Exchange(count, me, normed_slots, recv_normed, normed_out, normed_in)

    @pl.when(k == 0)
    def _():
        picked = dot(hot_columns(rim_col[...], rows), feats[...]).astype(BF16)
        rim_send[0] = picked[:rim]
        rim_send[1] = picked[rim:]
        greet([lax.rem(me + step, count) for step in range(1, count)])
        to_before.start()
        to_after.start()
        put_slots(grad_slots, dot(hot_rows(slot_row[...], slots), grads[...]).astype(BF16))
        grad_swap.start()
        table[:, :rows] = feats[...].T
        acc[...] = jnp.zeros_like(acc)
        to_before.wait_recv()
        to_after.wait_recv()
        low = jnp.where(me > 0, 1.0, 0.0) * rim_recv[0].astype(F32)
        high = jnp.where(me < count - 1, 1.0, 0.0) * rim_recv[1].astype(F32)
        table[:, rows : rows + rim] = low.T.astype(BF16)
        table[:, rows + rim :] = high.T.astype(BF16)
        to_before.wait_send()
        to_after.wait_send()

    total = acc[...]
    for one in range(nbrs.shape[0]):
        gathered = dot(table[...], hot_rows(nbrs[one], rows + 2 * rim)).astype(BF16)
        gathered_out[one] = gathered
        total += dot(weight[one], gathered, 0, 0)
    acc[...] = total

    @pl.when(k == pl.num_programs(0) - 1)
    def _():
        hidden = feats[...].astype(F32) + acc[...].T
        hidden_out[...] = hidden
        standard, _ = normalise(hidden)
        normed = (standard * gain[...]).astype(BF16)
        put_slots(normed_slots, dot(hot_rows(slot_row[...], slots), normed).astype(BF16))
        normed_swap.start()
        grad_swap.arrive()
        grad_swap.leave()
        normed_swap.arrive()
        normed_swap.leave()


def attention_kernel(
    count, recv_normed, recv_grad, rows_row, rows_col, qkv_w, proj_w,
    out_proj, back_grad, qkv_term, proj_term,
    qkv_t, scaled_t, up_t, att_t, grad_t, grad_slots, sent, received,
):
    me = lax.axis_index("gx")
    swap = Exchange(count, me, grad_slots, back_grad, sent, received)
    channels = proj_w.shape[0]
    slots = recv_normed.shape[0]
    picks = hot_columns(rows_col[...], slots)
    patch_in = dot(picks, recv_normed[...]).astype(BF16)
    patch_grad = dot(picks, recv_grad[...]).astype(BF16)
    qkv = dot(patch_in, qkv_w[...]).T
    qkv_t[...] = qkv.astype(BF16)
    scaled_t[...] = (qkv_t[:channels, :].astype(F32) * 0.25).astype(BF16)
    up_t[...] = dot(patch_grad, proj_w[...], 1, 1).T.astype(BF16)

    def head(h, carry):
        def part(ref, base=0):
            return ref[pl.ds(pl.multiple_of(base + h * HEAD, HEAD), HEAD), :]

        query, keys, values = part(qkv_t), part(qkv_t, channels), part(qkv_t, 2 * channels)
        query_low = part(scaled_t)
        up = part(up_t)
        up_low = (up.astype(F32) * 0.25).astype(BF16)
        scores = dot(keys, query_low, 0, 0)
        raised = jnp.exp(scores - jnp.max(scores, axis=0, keepdims=True))
        probs = raised * (1.0 / jnp.sum(raised, axis=0, keepdims=True))
        probs_low = probs.astype(BF16)
        grad_probs = dot(values, up_low, 0, 0)
        total = jnp.sum(grad_probs * probs, axis=0, keepdims=True)
        grad_scores = (probs * (grad_probs - total)).astype(BF16)

        def put(ref, value, base=0):
            ref[pl.ds(pl.multiple_of(base + h * HEAD, HEAD), HEAD), :] = value.astype(BF16)

        put(att_t, dot(values, probs_low))
        put(grad_t, dot(up, probs_low, 1, 1), 2 * channels)
        put(grad_t, dot(keys, grad_scores))
        put(grad_t, dot(query, grad_scores, 1, 1), channels)
        return carry

    lax.fori_loop(0, HEADS, head, 0, unroll=2)
    back = hot_rows(rows_row[...], slots)
    grad_qkv = grad_t[...].astype(F32).T.astype(BF16)
    grad_normed = dot(grad_qkv, qkv_w[...], 1, 1).astype(BF16)
    put_slots(grad_slots, dot(back, grad_normed).astype(BF16))
    greet([lax.rem(me + step, count) for step in range(1, count)])
    swap.start()
    proj_out = dot(att_t[...], proj_w[...], 0, 0).astype(BF16)
    out_proj[...] = dot(back, proj_out).astype(BF16)
    proj_term[...] = dot(att_t[...], patch_grad)
    qkv_term[...] = dot(patch_in, grad_qkv, 0, 0)
    swap.arrive()
    swap.leave()


def backward_kernel(
    count, gain_row, hidden, proj_slots, back_grad, out_grad, gain, slot_col, small, gathered,
    block_out, total_out,
    grad_hidden, columns, proj_back, near_send, near_recv, mid_send, mid_recv, far_send, far_recv,
    load, proj_sent, proj_got, near_sent, near_got, mid_sent, mid_got, far_sent, far_got,
):
    me = lax.axis_index("gx")
    core = lax.rem(me, 2)
    chip = me // 2
    side = lax.rem(chip, 2)
    group = chip // 2
    groups = count // 4
    conv_rows = columns.shape[1]
    order = [lax.rem(group + step, groups) for step in range(1, groups + 1)]

    def device(of_group, of_side, of_core):
        return of_group * 4 + of_side * 2 + of_core

    loading = pltpu.make_async_copy(gathered, columns, load.at[0])
    loading.start()
    greet([lax.rem(me + step, count) for step in range(1, count)])
    proj_swap = Exchange(count, me, proj_slots, proj_back, proj_sent, proj_got)
    proj_swap.start()

    picks = hot_columns(slot_col[...], back_grad.shape[0])
    grad_back = dot(picks, back_grad[...])
    standard, inv_std = normalise(hidden[...])
    gain_term = jnp.sum(grad_back * standard, axis=0, keepdims=True)
    scaled = grad_back * gain[...]
    grad_hidden[...] = (
        out_grad[...].astype(F32)
        + inv_std
        * (
            scaled
            - jnp.mean(scaled, axis=-1, keepdims=True)
            - standard * jnp.mean(scaled * standard, axis=-1, keepdims=True)
        )
    ).astype(BF16)
    small_rows, channels = small.shape[1:]
    at_row = lax.broadcasted_iota(jnp.int32, (small_rows, channels), 0)
    gain_part = jnp.where(at_row == gain_row, 1.0, 0.0) * gain_term
    loading.wait()

    near = []
    for step, other in enumerate(order):
        for part, of_side in enumerate((1 - side, side)):
            place = 2 * step + part
            theirs = device(other, of_side, 1 - core)
            near_send[place, :conv_rows] = dot(columns[theirs], grad_hidden[...])
            near_send[place, conv_rows:] = small[theirs] + gain_part
            one = copy_to(near_send.at[place], near_recv.at[place], near_sent.at[place],
                          near_got.at[place], device(group, side, 1 - core))
            one.start()
            near.append(one)

    def both_cores(place, mine):
        conv = dot(columns[mine], grad_hidden[...])
        near[place].wait_recv()
        return (
            conv + near_recv[place, :conv_rows],
            small[mine] + gain_part + near_recv[place, conv_rows:],
        )

    mid = []
    for step, other in enumerate(order):
        conv, rest = both_cores(2 * step, device(other, 1 - side, core))
        mid_send[step, :conv_rows] = conv.astype(BF16)
        mid_send[step, conv_rows:] = rest.astype(BF16)
        one = copy_to(mid_send.at[step], mid_recv.at[step], mid_sent.at[step], mid_got.at[step],
                      device(group, 1 - side, core))
        one.start()
        mid.append(one)
    far = []
    for step, other in enumerate(order):
        conv, rest = both_cores(2 * step + 1, device(other, side, core))
        mid[step].wait_recv()
        conv += mid_recv[step, :conv_rows].astype(F32)
        rest += mid_recv[step, conv_rows:].astype(F32)
        if step < groups - 1:
            far_send[step, :conv_rows] = conv.astype(BF16)
            far_send[step, conv_rows:] = rest.astype(BF16)
            one = copy_to(far_send.at[step], far_recv.at[step], far_sent.at[step],
                          far_got.at[step], device(other, side, core))
            one.start()
            far.append(one)
        else:
            total_out[:conv_rows] = conv
            total_out[conv_rows:] = rest
    proj_swap.arrive()
    back_proj = dot(picks, proj_back[...].reshape(back_grad.shape))
    block_out[...] = (hidden[...] + back_proj).astype(BF16)
    for step in range(groups - 1):
        far[step].wait_recv()
        total_out[...] += far_recv[step].astype(F32)
    proj_swap.leave()
    for one in near + mid + far:
        one.wait_send()


def params(**more):
    return pltpu.CompilerParams(vmem_limit_bytes=LIMIT, **more)


def shape(dims, dtype):
    return jax.ShapeDtypeStruct(dims, dtype)


def on_device(
    features,
    neighbours,
    rim_rows,
    tile_slot,
    patch_rows,
    conv_weight,
    norm_gain,
    qkv_weight,
    proj_weight,
    out_grad,
):
    rows, channels = features.shape
    count = lax.axis_size("gx")
    capacity = 2 * rows // count
    slots = count * capacity
    rim = rim_rows.shape[0] // 2
    kernel = neighbours.shape[0]
    gain = norm_gain.reshape(1, channels)
    slot_row, slot_col = tile_slot.reshape(1, rows), tile_slot.reshape(rows, 1)
    rows_row, rows_col = patch_rows.reshape(1, rows), patch_rows.reshape(rows, 1)

    def full(*dims):
        return pl.BlockSpec(dims, lambda k: (0,) * len(dims))

    def dma(size):
        return pltpu.SemaphoreType.DMA((size,))

    anywhere = pl.BlockSpec(memory_space=pl.ANY)
    blocks = (count, capacity, channels)
    each = 9 if kernel % 9 == 0 else 1
    gathered, hidden, recv_normed, recv_grad = pl.pallas_call(
        functools.partial(conv_kernel, count),
        grid=(kernel // each,),
        out_shape=(
            shape((kernel, channels, rows), BF16),
            shape((rows, channels), F32),
            shape(blocks, BF16),
            shape(blocks, BF16),
        ),
        in_specs=[
            full(rows, channels),
            full(rows, channels),
            full(2 * rim, 1),
            pl.BlockSpec((each, 1, rows), lambda k: (k, 0, 0)),
            pl.BlockSpec((each, channels, channels), lambda k: (k, 0, 0)),
            full(1, channels),
            full(1, rows),
        ],
        out_specs=(
            pl.BlockSpec((each, channels, rows), lambda k: (k, 0, 0)),
            full(rows, channels),
            anywhere,
            anywhere,
        ),
        scratch_shapes=[
            pltpu.VMEM((channels, rows + 2 * rim), BF16),
            pltpu.VMEM((channels, rows), F32),
            pltpu.VMEM((2, rim, channels), BF16),
            pltpu.VMEM((2, rim, channels), BF16),
            pltpu.VMEM(blocks, BF16),
            pltpu.VMEM(blocks, BF16),
            dma(2), dma(2), dma(count), dma(count), dma(count), dma(count),
        ],
        compiler_params=params(collective_id=1, has_side_effects=True),
        name="conv",
    )(
        features, out_grad, rim_rows.reshape(2 * rim, 1), neighbours.reshape(kernel, 1, rows),
        conv_weight.reshape(kernel, channels, channels), gain, slot_row,
    )

    proj_slots, back_grad, qkv_term, proj_term = pl.pallas_call(
        functools.partial(attention_kernel, count),
        out_shape=(
            shape((slots, channels), BF16),
            shape(blocks, BF16),
            shape((channels, 3 * channels), F32),
            shape((channels, channels), F32),
        ),
        in_specs=[VMEM] * 6,
        out_specs=(VMEM, anywhere, VMEM, VMEM),
        scratch_shapes=[
            pltpu.VMEM((3 * channels, rows), BF16),
            pltpu.VMEM((channels, rows), BF16),
            pltpu.VMEM((channels, rows), BF16),
            pltpu.VMEM((channels, rows), BF16),
            pltpu.VMEM((3 * channels, rows), BF16),
            pltpu.VMEM(blocks, BF16),
            dma(count), dma(count),
        ],
        compiler_params=params(collective_id=2, has_side_effects=True),
        name="attention",
    )(
        recv_normed.reshape(slots, channels), recv_grad.reshape(slots, channels),
        rows_row, rows_col, qkv_weight, proj_weight,
    )

    conv_rows = kernel * channels // count
    padded_rows = -(-conv_rows // 16) * 16
    one = channels // count
    gain_row = 4 * one
    small_rows = -(-(gain_row + 1) // 16) * 16
    small = jnp.concatenate(
        [
            qkv_term.reshape(count, 3 * one, channels),
            proj_term.reshape(count, one, channels),
            jnp.zeros((count, small_rows - gain_row, channels), F32),
        ],
        axis=1,
    )
    columns = gathered.reshape(count, conv_rows, rows)
    if padded_rows > conv_rows:
        columns = jnp.pad(columns, ((0, 0), (0, padded_rows - conv_rows), (0, 0)))
    chips, groups, chunk = count // 2, count // 4, padded_rows + small_rows
    block_out, total = pl.pallas_call(
        functools.partial(backward_kernel, count, gain_row),
        out_shape=(shape((rows, channels), BF16), shape((chunk, channels), F32)),
        in_specs=[VMEM] * 7 + [anywhere],
        out_specs=(VMEM, VMEM),
        scratch_shapes=[
            pltpu.VMEM((rows, channels), BF16),
            pltpu.VMEM((count, padded_rows, rows), BF16),
            pltpu.VMEM(blocks, BF16),
            pltpu.VMEM((chips, chunk, channels), F32),
            pltpu.VMEM((chips, chunk, channels), F32),
            pltpu.VMEM((groups, chunk, channels), BF16),
            pltpu.VMEM((groups, chunk, channels), BF16),
            pltpu.VMEM((groups - 1, chunk, channels), BF16),
            pltpu.VMEM((groups - 1, chunk, channels), BF16),
            dma(1), dma(count), dma(count), dma(chips), dma(chips),
            dma(groups), dma(groups), dma(groups), dma(groups),
        ],
        compiler_params=params(collective_id=3, has_side_effects=True),
        name="backward",
    )(
        hidden, proj_slots.reshape(blocks), back_grad.reshape(slots, channels), out_grad, gain,
        slot_col, small, columns,
    )
    small_sum = total[padded_rows:]
    return (
        block_out,
        total[:conv_rows],
        small_sum[: 3 * one].reshape(one, 3 * channels),
        small_sum[3 * one : gain_row],
        lax.dynamic_slice_in_dim(small_sum[gain_row], lax.axis_index("gx") * one, one),
    )


def solution(mesh):
    placed = (
        P(("parts", "gx"), None),
        P(None, ("parts", "gx")),
        P(("parts", "gx")),
        P(("parts", "gx")),
        P(("parts", "gx")),
        P(),
        P(),
        P(),
        P(),
        P(("parts", "gx"), None),
    )
    return jax.shard_map(
        on_device,
        mesh=mesh,
        in_specs=placed,
        out_specs=(
            P(("parts", "gx"), None),
            P(("parts", "gx"), None),
            P(("parts", "gx"), None),
            P(("parts", "gx"), None),
            P(("parts", "gx")),
        ),
        check_vma=False,
    )
```

```python
import functools

import jax
import jax.numpy as jnp
from jax import lax
from jax.experimental import pallas as pl
from jax.experimental.pallas import tpu as pltpu
from jax.sharding import PartitionSpec as P

HEADS = 16
HEAD = 16
LIMIT = 56 * 1024 * 1024
F32 = jnp.float32
BF16 = jnp.bfloat16
VMEM = pl.BlockSpec(memory_space=pltpu.VMEM)


def dot(a, b, ca=1, cb=0):
    return lax.dot_general(a, b, (((ca,), (cb,)), ((), ())), preferred_element_type=F32)


def hot_rows(index_row, count):
    rows = lax.broadcasted_iota(jnp.int32, (count, index_row.shape[1]), 0)
    return jnp.where(rows == index_row, 1.0, 0.0).astype(BF16)


def hot_columns(index_row, count):
    wide = jnp.broadcast_to(index_row.astype(F32), (8, index_row.shape[1]))
    index_column = wide.T[:, :1].astype(jnp.int32)
    columns = lax.broadcasted_iota(jnp.int32, (index_column.shape[0], count), 1)
    return jnp.where(columns == index_column, 1.0, 0.0).astype(BF16)


def normalise(hidden):
    centred = hidden - jnp.mean(hidden, axis=-1, keepdims=True)
    inv_std = 1.0 / jnp.sqrt(jnp.mean(centred * centred, axis=-1, keepdims=True) + 1e-05)
    return centred * inv_std, inv_std


def copy_to(source, target, send, recv, device):
    return pltpu.make_async_remote_copy(
        src_ref=source,
        dst_ref=target,
        send_sem=send,
        recv_sem=recv,
        device_id={"gx": device},
        device_id_type=pl.DeviceIdType.MESH,
    )


def greet(devices):
    barrier = pltpu.get_barrier_semaphore()
    for device in devices:
        pl.semaphore_signal(
            barrier, inc=1, device_id={"gx": device}, device_id_type=pl.DeviceIdType.MESH
        )
    pl.semaphore_wait(barrier, len(devices))


class Exchange:
    def __init__(self, count, me, source, target, send, recv):
        self.own = pltpu.make_async_copy(source.at[me], target.at[me], send.at[0])
        self.sends = []
        self.recvs = []
        for step in sorted(range(1, count), key=lambda step: abs(2 * step - count)):
            peer = lax.rem(me + step, count)
            sender = lax.rem(me + count - step, count)
            self.sends.append(
                copy_to(source.at[peer], target.at[me], send.at[step], recv.at[step], peer)
            )
            self.recvs.append(
                copy_to(source.at[peer], target.at[sender], send.at[step], recv.at[step], peer)
            )

    def start(self):
        for one in self.sends:
            one.start()
        self.own.start()

    def arrive(self):
        self.own.wait()
        for one in self.recvs:
            one.wait_recv()

    def leave(self):
        for one in self.sends:
            one.wait_send()


def put_slots(target, values):
    for block in range(target.shape[0]):
        cap = target.shape[1]
        target[block] = values[block * cap : (block + 1) * cap]


def conv_kernel(
    count, feats, grads, rim_row, nbrs, weight, gain, slot_row,
    gathered_out, hidden_out, recv_normed, recv_grad,
    table, acc, rim_send, rim_recv, grad_slots, normed_slots,
    rim_out, rim_in, grad_out, grad_in, normed_out, normed_in,
):
    k = pl.program_id(0)
    rows, channels = feats.shape
    rim = rim_recv.shape[1]
    each = weight.shape[0]
    slots = count * grad_slots.shape[1]
    me = lax.axis_index("gx")
    before, after = lax.rem(me + count - 1, count), lax.rem(me + 1, count)
    to_before = copy_to(rim_send.at[0], rim_recv.at[1], rim_out.at[0], rim_in.at[1], before)
    to_after = copy_to(rim_send.at[1], rim_recv.at[0], rim_out.at[1], rim_in.at[0], after)
    grad_swap = Exchange(count, me, grad_slots, recv_grad, grad_out, grad_in)
    normed_swap = Exchange(count, me, normed_slots, recv_normed, normed_out, normed_in)

    @pl.when(k == 0)
    def _():
        picked = dot(hot_columns(rim_row[...], rows), feats[...]).astype(BF16)
        rim_send[0] = picked[:rim]
        rim_send[1] = picked[rim:]
        greet([lax.rem(me + step, count) for step in range(1, count)])
        to_before.start()
        to_after.start()
        put_slots(grad_slots, dot(hot_rows(slot_row[...], slots), grads[...]).astype(BF16))
        grad_swap.start()
        table[:, :rows] = feats[...].T
        acc[...] = jnp.zeros_like(acc)
        to_before.wait_recv()
        to_after.wait_recv()
        low = jnp.where(me > 0, 1.0, 0.0) * rim_recv[0].astype(F32)
        high = jnp.where(me < count - 1, 1.0, 0.0) * rim_recv[1].astype(F32)
        table[:, rows : rows + rim] = low.T.astype(BF16)
        table[:, rows + rim :] = high.T.astype(BF16)
        to_before.wait_send()
        to_after.wait_send()

    total = acc[...]
    for one in range(each):
        gathered = dot(table[...], hot_rows(nbrs[pl.ds(k * each + one, 1), :], rows + 2 * rim)).astype(BF16)
        gathered_out[one] = gathered
        total += dot(weight[one], gathered, 0, 0)
    acc[...] = total

    @pl.when(k == pl.num_programs(0) - 1)
    def _():
        hidden = feats[...].astype(F32) + acc[...].T
        hidden_out[...] = hidden
        standard, _ = normalise(hidden)
        normed = (standard * gain[...]).astype(BF16)
        put_slots(normed_slots, dot(hot_rows(slot_row[...], slots), normed).astype(BF16))
        normed_swap.start()
        grad_swap.arrive()
        grad_swap.leave()
        normed_swap.arrive()
        normed_swap.leave()


def attention_kernel(
    count, recv_normed, recv_grad, rows_row, qkv_w, proj_w,
    out_proj, back_grad, qkv_term, proj_term,
    qkv_t, scaled_t, up_t, att_t, grad_t, grad_slots, sent, received,
):
    me = lax.axis_index("gx")
    swap = Exchange(count, me, grad_slots, back_grad, sent, received)
    channels = proj_w.shape[0]
    slots = recv_normed.shape[0]
    picks = hot_columns(rows_row[...], slots)
    patch_in = dot(picks, recv_normed[...]).astype(BF16)
    patch_grad = dot(picks, recv_grad[...]).astype(BF16)
    qkv = dot(patch_in, qkv_w[...]).T
    qkv_t[...] = qkv.astype(BF16)
    scaled_t[...] = (qkv_t[:channels, :].astype(F32) * 0.25).astype(BF16)
    up_t[...] = dot(patch_grad, proj_w[...], 1, 1).T.astype(BF16)

    def head(h, carry):
        def part(ref, base=0):
            return ref[pl.ds(pl.multiple_of(base + h * HEAD, HEAD), HEAD), :]

        query, keys, values = part(qkv_t), part(qkv_t, channels), part(qkv_t, 2 * channels)
        query_low = part(scaled_t)
        up = part(up_t)
        up_low = (up.astype(F32) * 0.25).astype(BF16)
        scores = dot(keys, query_low, 0, 0)
        raised = jnp.exp(scores - jnp.max(scores, axis=0, keepdims=True))
        probs = raised * (1.0 / jnp.sum(raised, axis=0, keepdims=True))
        probs_low = probs.astype(BF16)
        grad_probs = dot(values, up_low, 0, 0)
        total = jnp.sum(grad_probs * probs, axis=0, keepdims=True)
        grad_scores = (probs * (grad_probs - total)).astype(BF16)

        def put(ref, value, base=0):
            ref[pl.ds(pl.multiple_of(base + h * HEAD, HEAD), HEAD), :] = value.astype(BF16)

        put(att_t, dot(values, probs_low))
        put(grad_t, dot(up, probs_low, 1, 1), 2 * channels)
        put(grad_t, dot(keys, grad_scores))
        put(grad_t, dot(query, grad_scores, 1, 1), channels)
        return carry

    lax.fori_loop(0, HEADS, head, 0, unroll=4)
    back = hot_rows(rows_row[...], slots)
    grad_qkv = grad_t[...].astype(F32).T.astype(BF16)
    grad_normed = dot(grad_qkv, qkv_w[...], 1, 1).astype(BF16)
    put_slots(grad_slots, dot(back, grad_normed).astype(BF16))
    greet([lax.rem(me + step, count) for step in range(1, count)])
    swap.start()
    proj_out = dot(att_t[...], proj_w[...], 0, 0).astype(BF16)
    out_proj[...] = dot(back, proj_out).astype(BF16)
    proj_term[...] = dot(att_t[...], patch_grad)
    qkv_term[...] = dot(patch_in, grad_qkv, 0, 0)
    swap.arrive()
    swap.leave()


def backward_kernel(
    count, hidden, proj_slots, back_grad, out_grad, gain, slot_row, qkv_term, proj_term, gathered,
    block_out, conv_out, qkv_out, proj_out, gain_out,
    grad_hidden, columns, proj_back,
    near_send, near_recv, mid_send, mid_recv, far_send, far_recv,
    mid_small, mid_small_in, far_small, far_small_in, small_sum,
    load, proj_sent, proj_got, near_sent, near_got, mid_sent, mid_got, far_sent, far_got,
):
    me = lax.axis_index("gx")
    core = lax.rem(me, 2)
    chip = me // 2
    side = lax.rem(chip, 2)
    group = chip // 2
    groups = count // 4
    conv_rows = columns.shape[1]
    order = [lax.rem(group + step, groups) for step in range(1, groups + 1)]

    def device(of_group, of_side, of_core):
        return of_group * 4 + of_side * 2 + of_core

    loading = pltpu.make_async_copy(gathered, columns, load.at[0])
    loading.start()
    greet([lax.rem(me + step, count) for step in range(1, count)])
    proj_swap = Exchange(count, me, proj_slots, proj_back, proj_sent, proj_got)
    proj_swap.start()

    picks = hot_columns(slot_row[...], back_grad.shape[0])
    grad_back = dot(picks, back_grad[...])
    standard, inv_std = normalise(hidden[...])
    gain_term = jnp.sum(grad_back * standard, axis=0, keepdims=True)
    scaled = grad_back * gain[...]
    grad_hidden[...] = (
        out_grad[...].astype(F32)
        + inv_std
        * (
            scaled
            - jnp.mean(scaled, axis=-1, keepdims=True)
            - standard * jnp.mean(scaled * standard, axis=-1, keepdims=True)
        )
    ).astype(BF16)
    each, channels = proj_term.shape[1:]
    at_row = lax.broadcasted_iota(jnp.int32, (small_sum.shape[0] - 4 * each, channels), 0)
    gain_part = jnp.where(at_row == 0, 1.0, 0.0) * gain_term

    def put_small(target, base, mine, added=None):
        def put(low, high, value):
            target[base + low : base + high] = (
                value if added is None else value + added[conv_rows + low : conv_rows + high]
            )

        for third in range(3):
            block = qkv_term[mine, :, third * channels : (third + 1) * channels]
            put(third * each, (third + 1) * each, block)
        put(3 * each, 4 * each, proj_term[mine])
        put(4 * each, small_sum.shape[0], gain_part)

    loading.wait()

    near = []
    for step, other in enumerate(order):
        for part, of_side in enumerate((1 - side, side)):
            place = 2 * step + part
            theirs = device(other, of_side, 1 - core)
            near_send[place, :conv_rows] = dot(columns[theirs], grad_hidden[...])
            put_small(near_send.at[place], conv_rows, theirs)
            one = copy_to(near_send.at[place], near_recv.at[place], near_sent.at[place],
                          near_got.at[place], device(group, side, 1 - core))
            one.start()
            near.append(one)

    def both_cores(place, mine, small):
        conv = dot(columns[mine], grad_hidden[...])
        near[place].wait_recv()
        put_small(small, 0, mine, near_recv.at[place])
        return conv + near_recv[place, :conv_rows]

    mid, mid_f32 = [], []
    for step, other in enumerate(order):
        conv = both_cores(2 * step, device(other, 1 - side, core), mid_small.at[step])
        mid_send[step] = conv.astype(BF16)
        peer = device(group, 1 - side, core)
        mid.append(copy_to(mid_send.at[step], mid_recv.at[step], mid_sent.at[2 * step],
                           mid_got.at[2 * step], peer))
        mid_f32.append(copy_to(mid_small.at[step], mid_small_in.at[step],
                               mid_sent.at[2 * step + 1], mid_got.at[2 * step + 1], peer))
        mid[-1].start()
        mid_f32[-1].start()
    far, far_f32 = [], []
    for step, other in enumerate(order):
        conv = both_cores(2 * step + 1, device(other, side, core), small_sum)
        mid[step].wait_recv()
        mid_f32[step].wait_recv()
        conv += mid_recv[step].astype(F32)
        if step < groups - 1:
            far_send[step] = conv.astype(BF16)
            far_small[step] = small_sum[...] + mid_small_in[step]
            peer = device(other, side, core)
            far.append(copy_to(far_send.at[step], far_recv.at[step], far_sent.at[2 * step],
                               far_got.at[2 * step], peer))
            far_f32.append(copy_to(far_small.at[step], far_small_in.at[step],
                                   far_sent.at[2 * step + 1], far_got.at[2 * step + 1], peer))
            far[-1].start()
            far_f32[-1].start()
        else:
            conv_out[...] = conv
            small_sum[...] += mid_small_in[step]
    proj_swap.arrive()
    back_proj = dot(picks, proj_back[...].reshape(back_grad.shape))
    block_out[...] = (hidden[...] + back_proj).astype(BF16)
    for step in range(groups - 1):
        far[step].wait_recv()
        far_f32[step].wait_recv()
        conv_out[...] += far_recv[step].astype(F32)
        small_sum[...] += far_small_in[step]
    for third in range(3):
        block = small_sum[third * each : (third + 1) * each]
        qkv_out[:, third * channels : (third + 1) * channels] = block
    proj_out[...] = small_sum[3 * each : 4 * each]
    gain_out[...] = small_sum[4 * each : 4 * each + 1]
    proj_swap.leave()
    for one in near + mid + mid_f32 + far + far_f32:
        one.wait_send()


def params(**more):
    return pltpu.CompilerParams(vmem_limit_bytes=LIMIT, **more)


def shape(dims, dtype):
    return jax.ShapeDtypeStruct(dims, dtype)


def on_device(
    features,
    neighbours,
    rim_rows,
    tile_slot,
    patch_rows,
    conv_weight,
    norm_gain,
    qkv_weight,
    proj_weight,
    out_grad,
):
    rows, channels = features.shape
    count = lax.axis_size("gx")
    capacity = 2 * rows // count
    slots = count * capacity
    rim = rim_rows.shape[0] // 2
    kernel = neighbours.shape[0]
    gain = norm_gain.reshape(1, channels)
    slot_row, rows_row = tile_slot.reshape(1, rows), patch_rows.reshape(1, rows)

    def full(*dims):
        return pl.BlockSpec(dims, lambda k: (0,) * len(dims))

    def dma(size):
        return pltpu.SemaphoreType.DMA((size,))

    anywhere = pl.BlockSpec(memory_space=pl.ANY)
    blocks = (count, capacity, channels)
    each = 9 if kernel % 9 == 0 else 1
    gathered, hidden, recv_normed, recv_grad = pl.pallas_call(
        functools.partial(conv_kernel, count),
        grid=(kernel // each,),
        out_shape=(
            shape((kernel, channels, rows), BF16),
            shape((rows, channels), F32),
            shape(blocks, BF16),
            shape(blocks, BF16),
        ),
        in_specs=[
            full(rows, channels),
            full(rows, channels),
            full(1, 2 * rim),
            full(kernel, rows),
            pl.BlockSpec((each, channels, channels), lambda k: (k, 0, 0)),
            full(1, channels),
            full(1, rows),
        ],
        out_specs=(
            pl.BlockSpec((each, channels, rows), lambda k: (k, 0, 0)),
            full(rows, channels),
            anywhere,
            anywhere,
        ),
        scratch_shapes=[
            pltpu.VMEM((channels, rows + 2 * rim), BF16),
            pltpu.VMEM((channels, rows), F32),
            pltpu.VMEM((2, rim, channels), BF16),
            pltpu.VMEM((2, rim, channels), BF16),
            pltpu.VMEM(blocks, BF16),
            pltpu.VMEM(blocks, BF16),
            dma(2), dma(2), dma(count), dma(count), dma(count), dma(count),
        ],
        compiler_params=params(collective_id=1, has_side_effects=True),
        name="conv",
    )(
        features, out_grad, rim_rows.reshape(1, 2 * rim), neighbours,
        conv_weight.reshape(kernel, channels, channels), gain, slot_row,
    )

    proj_slots, back_grad, qkv_term, proj_term = pl.pallas_call(
        functools.partial(attention_kernel, count),
        out_shape=(
            shape((slots, channels), BF16),
            shape(blocks, BF16),
            shape((channels, 3 * channels), F32),
            shape((channels, channels), F32),
        ),
        in_specs=[VMEM] * 5,
        out_specs=(VMEM, anywhere, VMEM, VMEM),
        scratch_shapes=[
            pltpu.VMEM((3 * channels, rows), BF16),
            pltpu.VMEM((channels, rows), BF16),
            pltpu.VMEM((channels, rows), BF16),
            pltpu.VMEM((channels, rows), BF16),
            pltpu.VMEM((3 * channels, rows), BF16),
            pltpu.VMEM(blocks, BF16),
            dma(count), dma(count),
        ],
        compiler_params=params(collective_id=2, has_side_effects=True),
        name="attention",
    )(
        recv_normed.reshape(slots, channels), recv_grad.reshape(slots, channels),
        rows_row, qkv_weight, proj_weight,
    )

    conv_rows = kernel * channels // count
    padded_rows = -(-conv_rows // 16) * 16
    one = channels // count
    small_rows = -(-(4 * one + 1) // 8) * 8
    columns = gathered.reshape(count, conv_rows, rows)
    if padded_rows > conv_rows:
        columns = jnp.pad(columns, ((0, 0), (0, padded_rows - conv_rows), (0, 0)))
    chips, groups, chunk = count // 2, count // 4, padded_rows + small_rows
    block_out, conv_grad, qkv_grad, proj_grad, gain_sum = pl.pallas_call(
        functools.partial(backward_kernel, count),
        out_shape=(
            shape((rows, channels), BF16),
            shape((padded_rows, channels), F32),
            shape((one, 3 * channels), F32),
            shape((one, channels), F32),
            shape((1, channels), F32),
        ),
        in_specs=[VMEM] * 8 + [anywhere],
        out_specs=(VMEM,) * 5,
        scratch_shapes=[
            pltpu.VMEM((rows, channels), BF16),
            pltpu.VMEM((count, padded_rows, rows), BF16),
            pltpu.VMEM(blocks, BF16),
            pltpu.VMEM((chips, chunk, channels), F32),
            pltpu.VMEM((chips, chunk, channels), F32),
            pltpu.VMEM((groups, padded_rows, channels), BF16),
            pltpu.VMEM((groups, padded_rows, channels), BF16),
            pltpu.VMEM((groups - 1, padded_rows, channels), BF16),
            pltpu.VMEM((groups - 1, padded_rows, channels), BF16),
            pltpu.VMEM((groups, small_rows, channels), F32),
            pltpu.VMEM((groups, small_rows, channels), F32),
            pltpu.VMEM((groups - 1, small_rows, channels), F32),
            pltpu.VMEM((groups - 1, small_rows, channels), F32),
            pltpu.VMEM((small_rows, channels), F32),
            dma(1), dma(count), dma(count), dma(chips), dma(chips),
            dma(2 * groups), dma(2 * groups), dma(2 * groups), dma(2 * groups),
        ],
        compiler_params=params(collective_id=3, has_side_effects=True),
        name="backward",
    )(
        hidden, proj_slots.reshape(blocks), back_grad.reshape(slots, channels), out_grad, gain,
        slot_row, qkv_term.reshape(count, one, 3 * channels),
        proj_term.reshape(count, one, channels), columns,
    )
    return (
        block_out,
        conv_grad[:conv_rows],
        qkv_grad,
        proj_grad,
        lax.dynamic_slice_in_dim(gain_sum[0], lax.axis_index("gx") * one, one),
    )


def solution(mesh):
    placed = (
        P(("parts", "gx"), None),
        P(None, ("parts", "gx")),
        P(("parts", "gx")),
        P(("parts", "gx")),
        P(("parts", "gx")),
        P(),
        P(),
        P(),
        P(),
        P(("parts", "gx"), None),
    )
    return jax.shard_map(
        on_device,
        mesh=mesh,
        in_specs=placed,
        out_specs=(
            P(("parts", "gx"), None),
            P(("parts", "gx"), None),
            P(("parts", "gx"), None),
            P(("parts", "gx"), None),
            P(("parts", "gx")),
        ),
        check_vma=False,
    )
```
